256 devices in a mesh: dom: 64 (over z, x, core), rep: 4 (over y).
Axes of the slice: x: 4, y: 4, z: 8, core: 2. Of those that a mesh axis runs over, the one named last changes fastest.
Arguments:
- history: bfloat16 [131072, 256], P('dom'), may hold values from -6 to 6
- batch_ids: int32 [262144], P(('dom', 'rep')), may hold values from 0 to 2047
- halo_ids: int32 [256, 64, 32], P(('dom', 'rep')), may hold values from 0 to 2047
- halo_counts: int32 [256, 64], P(('dom', 'rep')), may hold values from 1 to 32, as said below
- adj_local: bfloat16 [262144, 1024], P(('dom', 'rep')), may hold values from -0.109375 to 0.109375
- adj_halo: bfloat16 [262144, 2048], P(('dom', 'rep')), may hold values from -0.109375 to 0.109375
- weight: bfloat16 [256, 256], replicated, may hold values from -0.375 to 0.375
- cotangent: bfloat16 [262144, 256], P(('dom', 'rep')), may hold values from -6 to 6
Outputs:
- layer_out: bfloat16 [262144, 256], P(('dom', 'rep'))
- grad_weight: float32 [256, 256], replicated
- history_grad: float32 [131072, 256], P('dom')
The draws below stay inside these ranges and needn't reach their ends.
Inputs may be any that keep to these rules, and one draw needn't show every extreme that they name: `halo_counts`: every device takes from every owner between 1 and 32 rows; for some owners every device takes exactly 32. `halo_ids`: rows of the owner's history; slots at or past the used count are unused. `batch_ids`: rows of the device's own partition's history; may repeat.
All inputs are finite; a program needn't handle non-finite values.
Results may differ from the reference program's by a relative error of at most 0.0065.
Values may be sent and summed in bfloat16 or wider, within the bound.
No kernel may reach another device: no remote copies, remote signals or barrier semaphores. Data moves between devices by JAX's collectives and lax.ppermute only.
A program may use at most 64 MiB of HBM per device.

```python
import jax
import jax.numpy as jnp
from jax import lax

H = 256
B = 1024
HR = 2048
CAP = 32
SLOTS = 2048
ROWS = 262144
NODES = 131072
N_DOM = 64
N_REP = 4


def draw_halo_counts(key, part):
    key = jax.random.fold_in(key, 7)
    key_counts, key_hot, key_pick = jax.random.split(key, 3)
    counts = jax.random.randint(key_counts, (N_DOM * N_REP, N_DOM), 1, CAP + 1)
    hot_owner = jax.random.randint(key_hot, (N_DOM,), 0, 4) == 0
    chosen = jax.random.randint(key_pick, (), 0, N_DOM)
    hot_owner = jnp.logical_or(hot_owner, jnp.arange(N_DOM) == chosen)
    return jnp.where(hot_owner[None, :], CAP, counts).astype(jnp.int32)


def with_ends(entries, key, low, top_value):
    longest = entries.shape.index(max(entries.shape))
    spots = []
    for shift in (0, 1):
        where = [jax.random.randint(jax.random.fold_in(key, axis), (), 0, length) for axis, length in enumerate(entries.shape)]
        where[longest] = (where[longest] + shift) % entries.shape[longest]
        spots.append(tuple(where))
    return entries.at[spots[0]].set(low).at[spots[1]].set(top_value)


def levels(rng, dims, cuts, low, high):
    def one(axis_at, parts):
        steps = jax.random.uniform(jax.random.fold_in(jax.random.fold_in(rng, 6), axis_at), (parts,), jnp.float32, low / len(cuts), high / len(cuts))
        return jnp.repeat(jnp.exp(steps), dims[axis_at] // parts).reshape((-1,) + (1,) * (len(dims) - axis_at - 1))

    level = one(*cuts[0])
    for cut in cuts[1:]:
        level = level * one(*cut)
    return level


def centred(rng, extent, spread, bound, cuts=(), held_as=jnp.bfloat16):
    drawn = jax.random.normal(rng, extent, jnp.float32) * spread
    if len(cuts) > 0:
        drawn = levels(rng, extent, cuts, -0.22, 0.18) * drawn
    return jnp.clip(drawn, min=-bound, max=bound).astype(held_as)


def setup_inputs(seed: int = 0) -> dict:
    seeds = jax.random.split(jax.random.key(seed), 9)
    history = centred(seeds[0], (NODES, H), 1.0, 6.0, ((0, 64),))
    batch_ids = with_ends(jax.random.randint(seeds[1], (ROWS,), 0, HR), jax.random.fold_in(seeds[1], 1), 0, HR - 1).astype(jnp.int32)
    halo_ids = with_ends(jax.random.randint(seeds[2], (N_DOM * N_REP, N_DOM, CAP), 0, HR), jax.random.fold_in(seeds[2], 1), 0, HR - 1).astype(jnp.int32)
    halo_counts = draw_halo_counts(jax.random.fold_in(seeds[8], 71), 0)
    adj_local = centred(seeds[4], (ROWS, B), (B + N_DOM * CAP) ** -0.5, 0.109375, ((0, 256),))
    adj_halo = centred(seeds[5], (ROWS, SLOTS), (B + N_DOM * CAP) ** -0.5, 0.109375, ((0, 256),))
    weight = centred(seeds[6], (H, H), H ** -0.5, 0.375)
    cotangent = centred(seeds[7], (ROWS, H), 1.0, 6.0, ((0, 256),))
    return {"history": history, "batch_ids": batch_ids, "halo_ids": halo_ids, "halo_counts": halo_counts, "adj_local": adj_local, "adj_halo": adj_halo, "weight": weight, "cotangent": cotangent}


def reference(history, batch_ids, halo_ids, halo_counts, adj_local, adj_halo, weight, cotangent):
    devices = N_DOM * N_REP

    def device_step(grad_table, device):
        owner = device // N_REP
        row_ids = lax.dynamic_slice_in_dim(batch_ids, device * B, B)
        inputs = history[owner * HR + row_ids]
        halo_local = lax.dynamic_index_in_dim(halo_ids, device, 0, keepdims=False)
        halo_global = (jnp.arange(N_DOM, dtype=jnp.int32)[:, None] * HR + halo_local).reshape(-1)
        halo_rows = history[halo_global]
        counts_row = lax.dynamic_index_in_dim(halo_counts, device, 0, keepdims=False)
        live_slots = (jnp.arange(CAP, dtype=jnp.int32)[None, :] < counts_row[:, None]).reshape(-1)
        local_adj = lax.dynamic_slice_in_dim(adj_local, device * B, B)
        halo_adj = lax.dynamic_slice_in_dim(adj_halo, device * B, B) * live_slots.astype(adj_halo.dtype)[None, :]
        cot_rows = lax.dynamic_slice_in_dim(cotangent, device * B, B)
        summed = jnp.dot(local_adj, inputs, preferred_element_type=jnp.float32) + jnp.dot(halo_adj, halo_rows, preferred_element_type=jnp.float32)
        agg = summed.astype(jnp.bfloat16)
        pre_act = jnp.dot(agg, weight, preferred_element_type=jnp.float32)
        gate_sig = jax.nn.sigmoid(pre_act)
        layer_rows = (pre_act * gate_sig).astype(jnp.bfloat16)
        grad_pre = (cot_rows.astype(jnp.float32) * gate_sig * (1.0 + pre_act * (1.0 - gate_sig))).astype(jnp.bfloat16)
        weight_part = jnp.dot(agg.T, grad_pre, preferred_element_type=jnp.float32)
        grad_agg = jnp.dot(grad_pre, weight.T, preferred_element_type=jnp.float32).astype(jnp.bfloat16)
        grad_inputs = jnp.dot(local_adj.T, grad_agg, preferred_element_type=jnp.float32).astype(jnp.bfloat16)
        grad_halo = jnp.dot(halo_adj.T, grad_agg, preferred_element_type=jnp.float32).astype(jnp.bfloat16)
        grad_table = grad_table.at[owner * HR + row_ids].add(grad_inputs.astype(jnp.float32))
        grad_table = grad_table.at[halo_global].add(grad_halo.astype(jnp.float32))
        return (grad_table, (layer_rows, weight_part))
    start_table = jnp.zeros((N_DOM * HR, H), jnp.float32)
    history_grad, (layer_parts, weight_parts) = lax.scan(device_step, start_table, jnp.arange(devices, dtype=jnp.int32))
    layer_out = layer_parts.reshape(devices * B, H)
    grad_weight = lax.optimization_barrier(jnp.sum(weight_parts, axis=0)) / jnp.sqrt(jnp.float32(ROWS))
    return (layer_out, grad_weight, history_grad)
```

```python
import jax
import jax.numpy as jnp
from jax import lax
from jax.experimental import pallas as pl
from jax.experimental.pallas import tpu as pltpu
from jax.sharding import PartitionSpec as P

BF16, F32, I32 = jnp.bfloat16, jnp.float32, jnp.int32
VMEM = pl.BlockSpec(memory_space=pltpu.VMEM)
SMEM = pl.BlockSpec(memory_space=pltpu.SMEM)
LOW = 4


def vmem_call(kernel, out_shape, in_specs, flops=0, moved=0, scratch=()):
    return pl.pallas_call(
        kernel,
        out_shape=out_shape,
        in_specs=in_specs,
        out_specs=jax.tree.map(lambda _: VMEM, out_shape),
        scratch_shapes=list(scratch),
        compiler_params=pltpu.CompilerParams(vmem_limit_bytes=40 * 1024 * 1024),
        cost_estimate=pl.CostEstimate(flops=flops, bytes_accessed=moved, transcendentals=0),
    )


def as_column(id_row):
    return jnp.broadcast_to(id_row, (128, 128)).T


def gather_kernel(ids_ref, table_ref, out_ref):
    nodes = table_ref.shape[0]
    lane = lax.broadcasted_iota(I32, (256, 128), 1)
    for step in range(out_ref.shape[0] // 256):
        column = jnp.concatenate(
            [as_column(ids_ref[2 * step : 2 * step + 1, :]), as_column(ids_ref[2 * step + 1 : 2 * step + 2, :])], 0
        )
        picks = jnp.concatenate(
            [(column == lane + base).astype(F32).astype(BF16) for base in range(0, nodes, 128)], 1
        )
        rows = jnp.dot(picks, table_ref[...], preferred_element_type=F32)
        out_ref[256 * step : 256 * step + 256, :] = rows.astype(BF16)


def gather_rows(table, ids):
    count, (nodes, width) = ids.shape[0], table.shape
    return vmem_call(
        gather_kernel,
        jax.ShapeDtypeStruct((count, width), BF16),
        [VMEM, VMEM],
        flops=2 * count * nodes * width,
        moved=4 * count * width,
    )(ids.reshape(count // 128, 128), table)


def pack_pair(first, second, part):
    block = slice(128 * (part // 2), 128 * (part // 2) + 128)
    left = lax.broadcasted_iota(I32, (first.shape[0], 128), 1) < 64
    if part % 2 == 0:
        return jnp.where(left, first[:, block], pltpu.roll(second[:, block], 64, 1))
    return jnp.where(left, pltpu.roll(first[:, block], 64, 1), second[:, block])


def pack_halo_kernel(counts_ref, grads_ref, weight_ref, out_ref):
    slots = 32
    row = lax.broadcasted_iota(I32, (slots, 256), 0)
    row8 = lax.broadcasted_iota(I32, (8, 128), 0) // 2
    for half in range(2):

        def one_owner(step, _, half=half):
            owner = step + 32 * half
            start = pl.multiple_of(owner * slots, slots)
            grads = jnp.where(row < counts_ref[0, owner], grads_ref[pl.ds(start, slots), :], 0.0)
            weights = weight_ref[pl.ds(pl.multiple_of(step * 8, 8), 8), 128 * half : 128 * half + 128]
            upper = weights.astype(BF16).astype(F32)
            lower = pltpu.roll(weights - upper, 4, 0)
            for part in range(4):
                tail = jnp.where(row8 == part, upper, jnp.where(row8 == (part + 2) % 4, lower, 0.0))
                message = jnp.concatenate([pack_pair(grads[:16], grads[16:], part), tail], 0)
                out_ref[owner * 4 + part] = message.astype(BF16)
            return 0

        lax.fori_loop(0, 32, one_owner, 0)


def pack_local_kernel(grads_ref, out_ref):
    half = grads_ref.shape[0] // 2
    for base in range(0, half, 64):
        first = grads_ref[base : base + 64, :]
        second = grads_ref[half + base : half + base + 64, :]
        for part in range(4):
            out_ref[part, base : base + 64, :] = pack_pair(first, second, part).astype(BF16)


def add_rows(total, first_ids, second_ids, first_low, second_low, packed):
    high_row = lax.broadcasted_iota(I32, (512, 128), 0)
    left = lax.broadcasted_iota(I32, (512, 128), 1) < 64
    group = jnp.where(left, 0, 1)
    wide = packed.astype(F32)
    turned = pltpu.roll(wide, 64, 1)
    for ids, low, rows in (
        (first_ids, first_low, jnp.where(left, wide, turned)),
        (second_ids, second_low, jnp.where(left, turned, wide)),
    ):
        spread = jnp.concatenate(
            [jnp.where(low == group, rows, 0.0), jnp.where(low == group + 2, rows, 0.0)], 1
        ).astype(BF16)
        picks = jnp.concatenate(
            [(high_row == (ids[i : i + 1, :] & 511)).astype(F32).astype(BF16) for i in range(4)], 1
        )
        total = total + jnp.dot(picks, spread, preferred_element_type=F32)
    return total


def scatter_local_kernel(first_ref, second_ref, first_low_ref, second_low_ref, *refs):
    packed_refs, out_ref = refs[:4], refs[4]
    total = jnp.zeros((512, 256), F32)
    for i, packed_ref in enumerate(packed_refs):
        k, n = slice(4 * i, 4 * i + 4), slice(512 * i, 512 * i + 512)
        total = add_rows(
            total, first_ref[k, :], second_ref[k, :], first_low_ref[n, :], second_low_ref[n, :], packed_ref[...]
        )
    out_ref[...] = total


def scatter_halo_kernel(first_ref, second_ref, first_low_ref, second_low_ref, packed_ref, start_ref, out_ref):
    total = start_ref[...]
    for i in range(8):
        k, n = slice(4 * i, 4 * i + 4), slice(512 * i, 512 * i + 512)
        packed = packed_ref[32 * i : 32 * i + 32, 0:16, :].reshape(512, 128)
        total = add_rows(
            total, first_ref[k, :], second_ref[k, :], first_low_ref[n, :], second_low_ref[n, :], packed
        )
    out_ref[...] = total.astype(BF16)


def unpack_kernel(rep_ref, *refs):
    tables, out_ref = refs[:4], refs[4]
    left = lax.broadcasted_iota(I32, (128, 128), 1) < 64
    for rep in range(4):

        @pl.when(rep_ref[0] == rep)
        def _(rep=rep):
            for low in range(4):
                for base in range(0, 512, 128):
                    block = [
                        tables[(rep - part) % 4][base : base + 128, 128 * (low // 2) : 128 * (low // 2) + 128].astype(F32)
                        for part in range(4)
                    ]
                    for pair in range(2):
                        one, two = block[2 * pair], block[2 * pair + 1]
                        if low % 2 == 0:
                            joined = jnp.where(left, one, pltpu.roll(two, 64, 1))
                        else:
                            joined = jnp.where(left, pltpu.roll(one, 64, 1), two)
                        out_ref[512 * low + base : 512 * low + base + 128, 128 * pair : 128 * pair + 128] = joined


def exchange(x, axes):
    return lax.all_to_all(x, axes, split_axis=0, concat_axis=0, tiled=True)


def from_behind(x, by):
    return lax.ppermute(x, "rep", [(i, (i + by) % 4) for i in range(4)])


def lows(ids):
    return jnp.broadcast_to((ids >> 9).reshape(-1, 1), (ids.size, 128))


def body(history, batch_ids, halo_ids, halo_counts, adj_local, adj_halo, weight, cotangent):
    owners = lax.axis_size("dom")
    replicas = lax.axis_size("rep")
    rep = lax.axis_index("rep")
    batch_rows = batch_ids.shape[0]
    slots = halo_ids.shape[2]
    width = history.shape[1]
    both = ("dom", "rep")

    asked = exchange(halo_ids.reshape(owners, 1, slots), "dom").reshape(owners * slots)
    fetched = gather_rows(history, asked)
    halo_rows = exchange(fetched.reshape(owners, slots, width), "dom").reshape(owners * slots, width)

    mine = jnp.concatenate([asked, batch_ids]).reshape(-1, 128)
    ids = [mine] + [from_behind(mine, by) for by in (1, 2, 3)]
    asked_rows = owners * slots // 128
    local_ids = jnp.stack([i[asked_rows:] for i in ids], 0).reshape(replicas, 2, batch_rows // 2)
    by_age = jnp.stack([i[:asked_rows] for i in ids[::-1]], 0)
    by_rep = jnp.roll(by_age, rep + 1, 0).reshape(replicas, owners, 2, slots // 2).transpose(2, 1, 0, 3)
    local_first, local_second = local_ids[:, 0].reshape(-1, 128), local_ids[:, 1].reshape(-1, 128)
    halo_first, halo_second = by_rep[0].reshape(-1, 128), by_rep[1].reshape(-1, 128)

    inputs = gather_rows(history, batch_ids)
    live = jnp.arange(slots, dtype=I32)[None, :] < halo_counts.reshape(owners, 1)
    live_rows = jnp.where(live.reshape(-1, 1), halo_rows, jnp.zeros((), BF16))
    summed = jnp.dot(adj_local, inputs, preferred_element_type=F32) + jnp.dot(
        adj_halo, live_rows, preferred_element_type=F32
    )
    agg = summed.astype(BF16)
    pre_act = jnp.dot(agg, weight, preferred_element_type=F32)
    gate = jax.nn.sigmoid(pre_act)
    layer_out = (pre_act * gate).astype(BF16)
    grad_pre = (cotangent.astype(F32) * gate * (1.0 + pre_act * (1.0 - gate))).astype(BF16)
    weight_part = lax.dot_general(agg, grad_pre, (((0,), (0,)), ((), ())), preferred_element_type=F32)
    grad_agg = lax.dot_general(grad_pre, weight, (((1,), (1,)), ((), ())), preferred_element_type=F32).astype(BF16)
    grad_halo = lax.dot_general(adj_halo, grad_agg, (((0,), (0,)), ((), ())), preferred_element_type=F32)

    messages = vmem_call(
        pack_halo_kernel,
        jax.ShapeDtypeStruct((owners * replicas, 24, 128), BF16),
        [SMEM, VMEM, VMEM],
        moved=4 * 2**20,
    )(halo_counts, grad_halo, weight_part)
    arrived = exchange(messages, both)

    grad_inputs = lax.dot_general(adj_local, grad_agg, (((0,), (0,)), ((), ())), preferred_element_type=F32)
    packed = vmem_call(
        pack_local_kernel,
        jax.ShapeDtypeStruct((replicas, batch_rows // 2, 128), BF16),
        [VMEM],
        moved=2 * 2**20,
    )(grad_inputs)
    locals_ = [lax.dynamic_index_in_dim(packed, rep, 0, keepdims=False)] + [
        from_behind(lax.dynamic_index_in_dim(packed, (rep + by) % replicas, 0, keepdims=False), by) for by in (1, 2, 3)
    ]
    part_shape = jax.ShapeDtypeStruct((512, 256), F32)
    started = vmem_call(scatter_local_kernel, part_shape, [VMEM] * 8, flops=2 * 4096 * 512 * 256, moved=4 * 2**20)(
        local_first, local_second, lows(local_first), lows(local_second), *locals_
    )
    table = vmem_call(
        scatter_halo_kernel,
        jax.ShapeDtypeStruct((512, 256), BF16),
        [VMEM] * 6,
        flops=2 * 8192 * 512 * 256,
        moved=6 * 2**20,
    )(halo_first, halo_second, lows(halo_first), lows(halo_second), arrived, started)
    tables = [table] + [from_behind(table, by) for by in (1, 2, 3)]
    history_grad = vmem_call(
        unpack_kernel,
        jax.ShapeDtypeStruct(history.shape, F32),
        [SMEM] + [VMEM] * 4,
        moved=4 * 2**20,
    )(rep.reshape(1), *tables)

    tails = jnp.sum(arrived[:, 16:, :].astype(F32), axis=0)
    tails = tails + jnp.roll(tails, 4, 0)
    own = lax.dynamic_slice_in_dim(tails, 2 * rep, 2, 0)
    everyone = exchange(jnp.broadcast_to(own[None], (owners * replicas, 2, 128)), both).reshape(2, 256, 128)
    total_rows = batch_rows * owners * replicas
    grad_weight = jnp.concatenate([everyone[0], everyone[1]], 1) / jnp.sqrt(jnp.float32(total_rows))
    return (layer_out, grad_weight, history_grad)


def solution(mesh):
    return jax.shard_map(
        body,
        mesh=mesh,
        in_specs=(
            P("dom", None),
            P(("dom", "rep")),
            P(("dom", "rep"), None, None),
            P(("dom", "rep"), None),
            P(("dom", "rep"), None),
            P(("dom", "rep"), None),
            P(),
            P(("dom", "rep"), None),
        ),
        out_specs=(P(("dom", "rep"), None), P(), P("dom", None)),
        check_vma=False,
    )
```

```python
import jax
import jax.numpy as jnp
from jax import lax
from jax.experimental import pallas as pl
from jax.experimental.pallas import tpu as pltpu
from jax.sharding import PartitionSpec as P

BF16, F32, I32 = jnp.bfloat16, jnp.float32, jnp.int32
VMEM = pl.BlockSpec(memory_space=pltpu.VMEM)
SMEM = pl.BlockSpec(memory_space=pltpu.SMEM)
LOW = 4


def vmem_call(kernel, out_shape, in_specs, flops=0, moved=0, scratch=()):
    return pl.pallas_call(
        kernel,
        out_shape=out_shape,
        in_specs=in_specs,
        out_specs=jax.tree.map(lambda _: VMEM, out_shape),
        scratch_shapes=list(scratch),
        compiler_params=pltpu.CompilerParams(vmem_limit_bytes=16 * 1024 * 1024),
        cost_estimate=pl.CostEstimate(flops=flops, bytes_accessed=moved, transcendentals=0),
    )


def as_column(id_row):
    return jnp.broadcast_to(id_row, (128, 128)).T


def gather_kernel(ids_ref, table_ref, out_ref):
    nodes = table_ref.shape[0]
    lane = lax.broadcasted_iota(I32, (256, 128), 1)
    for step in range(out_ref.shape[0] // 256):
        column = jnp.concatenate(
            [as_column(ids_ref[2 * step : 2 * step + 1, :]), as_column(ids_ref[2 * step + 1 : 2 * step + 2, :])], 0
        )
        picks = jnp.concatenate(
            [(column == lane + base).astype(F32).astype(BF16) for base in range(0, nodes, 128)], 1
        )
        rows = jnp.dot(picks, table_ref[...], preferred_element_type=F32)
        out_ref[256 * step : 256 * step + 256, :] = rows.astype(BF16)


def gather_rows(table, ids):
    count, (nodes, width) = ids.shape[0], table.shape
    return vmem_call(
        gather_kernel,
        jax.ShapeDtypeStruct((count, width), BF16),
        [VMEM, VMEM],
        flops=2 * count * nodes * width,
        moved=4 * count * width,
    )(ids.reshape(count // 128, 128), table)


def pack_pair(first, second, part):
    block = slice(128 * (part // 2), 128 * (part // 2) + 128)
    left = lax.broadcasted_iota(I32, (first.shape[0], 128), 1) < 64
    if part % 2 == 0:
        return jnp.where(left, first[:, block], pltpu.roll(second[:, block], 64, 1))
    return jnp.where(left, pltpu.roll(first[:, block], 64, 1), second[:, block])


def middle_kernel(
    counts_ref, rows_ref, adj_ref, local_ref, weight_ref, cotangent_ref,
    out_ref, part_ref, grads_ref, messages_ref, live_ref, agg_ref, grad_pre_ref,
):
    slots, owners = 32, 64
    slot = lax.broadcasted_iota(I32, (slots, 256), 0)
    for owner in range(owners):
        at = slice(slots * owner, slots * owner + slots)
        live = jnp.where(slot < counts_ref[0, owner], rows_ref[at, :].astype(F32), 0.0)
        live_ref[at, :] = live.astype(BF16)
    for base in range(0, out_ref.shape[0], 256):
        at = slice(base, base + 256)
        summed = local_ref[at, :] + jnp.dot(adj_ref[at, :], live_ref[...], preferred_element_type=F32)
        agg = summed.astype(BF16)
        agg_ref[at, :] = agg
        pre_act = jnp.dot(agg, weight_ref[...], preferred_element_type=F32)
        gate = jax.nn.sigmoid(pre_act)
        out_ref[at, :] = (pre_act * gate).astype(BF16)
        grad_pre = (cotangent_ref[at, :].astype(F32) * gate * (1.0 + pre_act * (1.0 - gate))).astype(BF16)
        grad_pre_ref[at, :] = grad_pre
        grads_ref[at, :] = lax.dot_general(
            grad_pre, weight_ref[...], (((1,), (1,)), ((), ())), preferred_element_type=F32
        ).astype(BF16)
    part_ref[...] = lax.dot_general(
        agg_ref[...], grad_pre_ref[...], (((0,), (0,)), ((), ())), preferred_element_type=F32
    )
    for group in range(owners // 8):
        grads = lax.dot_general(
            adj_ref[:, 256 * group : 256 * group + 256],
            grads_ref[...],
            (((0,), (0,)), ((), ())),
            preferred_element_type=F32,
        )
        for step in range(8):
            owner = 8 * group + step
            one = jnp.where(slot < counts_ref[0, owner], grads[slots * step : slots * step + slots], 0.0)
            for part in range(4):
                messages_ref[owner * 4 + part] = pack_pair(one[:16], one[16:], part).astype(BF16)


def local_kernel(rep_ref, adj_ref, grads_ref, *refs):
    out_refs, sums_ref = refs[:4], refs[4]
    half = sums_ref.shape[0] // 2
    for base in range(0, 2 * half, 256):
        at = slice(base, base + 256)
        sums_ref[at, :] = lax.dot_general(
            adj_ref[:, at], grads_ref[...], (((0,), (0,)), ((), ())), preferred_element_type=F32
        )
    for rep in range(4):

        @pl.when(rep_ref[0] == rep)
        def _(rep=rep):
            for base in range(0, half, 128):
                first, second = sums_ref[base : base + 128, :], sums_ref[half + base : half + base + 128, :]
                for part in range(4):
                    out_refs[(part - rep) % 4][base : base + 128, :] = pack_pair(first, second, part).astype(BF16)


def picks_kernel(ids_ref, out_ref):
    high_row = lax.broadcasted_iota(I32, (512, 128), 0)
    for i in range(ids_ref.shape[0]):
        same = high_row == (ids_ref[i : i + 1, :] & 511)
        out_ref[:, 128 * i : 128 * i + 128] = same.astype(F32).astype(BF16)


def spread_rows(packed, first_low, second_low):
    left = lax.broadcasted_iota(I32, packed.shape, 1) < 64
    group = jnp.where(left, 0, 1)
    wide = packed.astype(F32)
    turned = pltpu.roll(wide, 64, 1)
    spread = []
    for low, rows in ((first_low, jnp.where(left, wide, turned)), (second_low, jnp.where(left, turned, wide))):
        spread.append(
            jnp.concatenate(
                [jnp.where(low == group, rows, 0.0), jnp.where(low == group + 2, rows, 0.0)], 1
            ).astype(BF16)
        )
    return spread


def scatter_local_kernel(picks_ref, low_ref, *refs):
    packed_refs, (out_ref, spread_ref) = refs[:4], refs[4:]
    for i, packed_ref in enumerate(packed_refs):
        n, m = slice(512 * i, 512 * i + 512), slice(2048 + 512 * i, 2048 + 512 * i + 512)
        spread_ref[n, :], spread_ref[m, :] = spread_rows(packed_ref[...], low_ref[n, :], low_ref[m, :])
    out_ref[...] = jnp.dot(picks_ref[...], spread_ref[...], preferred_element_type=F32)


def scatter_halo_kernel(picks_ref, low_ref, packed_ref, start_ref, out_ref, spread_ref):
    rows = packed_ref.shape[0]
    for base in range(0, rows, 512):
        n, m = slice(base, base + 512), slice(rows + base, rows + base + 512)
        spread_ref[n, :], spread_ref[m, :] = spread_rows(packed_ref[n, :], low_ref[n, :], low_ref[m, :])
    for base in range(0, 512, 256):
        at = slice(base, base + 256)
        total = start_ref[at, :] + jnp.dot(picks_ref[at, :], spread_ref[...], preferred_element_type=F32)
        out_ref[at, :] = total.astype(BF16)


def unpack_kernel(rep_ref, *refs):
    tables, out_ref = refs[:4], refs[4]
    left = lax.broadcasted_iota(I32, (128, 128), 1) < 64
    for rep in range(4):

        @pl.when(rep_ref[0] == rep)
        def _(rep=rep):
            for low in range(4):
                for base in range(0, 512, 128):
                    block = [
                        tables[(rep - part) % 4][base : base + 128, 128 * (low // 2) : 128 * (low // 2) + 128].astype(F32)
                        for part in range(4)
                    ]
                    for pair in range(2):
                        one, two = block[2 * pair], block[2 * pair + 1]
                        if low % 2 == 0:
                            joined = jnp.where(left, one, pltpu.roll(two, 64, 1))
                        else:
                            joined = jnp.where(left, pltpu.roll(one, 64, 1), two)
                        out_ref[512 * low + base : 512 * low + base + 128, 128 * pair : 128 * pair + 128] = joined


def exchange(x, axes):
    return lax.all_to_all(x, axes, split_axis=0, concat_axis=0, tiled=True)


def from_behind(x, by):
    return lax.ppermute(x, "rep", [(i, (i + by) % 4) for i in range(4)])


def lows(ids):
    return jnp.broadcast_to((ids >> 9).reshape(-1, 1), (ids.size, 128))


def picks(ids):
    return vmem_call(picks_kernel, jax.ShapeDtypeStruct((512, ids.size), BF16), [VMEM], moved=1024 * ids.size)(
        ids.reshape(-1, 128)
    )


def owner_shift(x, place):
    return lax.ppermute(x, "dom", [(i, place(i // 8, i // 2 % 4, i % 2)) for i in range(64)])


def rows_of(x, index, rows):
    return lax.dynamic_slice_in_dim(x, index * rows, rows, 0)


def in_order(parts, me):
    place = lax.broadcasted_iota(I32, (4,) + parts[0].shape, 0)
    stacked = jnp.zeros((), parts[0].dtype)
    for by, part in enumerate(parts):
        stacked = jnp.where(place == ((me - by) & 3), part[None], stacked)
    return stacked


def along(axis, x, by):
    if axis == "rep":
        return from_behind(x, by)
    if axis == "core":
        return owner_shift(x, lambda z, x, core: z * 8 + x * 2 + 1 - core)
    if axis == "x":
        return owner_shift(x, lambda z, x, core: z * 8 + (x + by) % 4 * 2 + core)
    return owner_shift(x, lambda z, x, core: (z ^ by) * 8 + x * 2 + core)


def place():
    dom = lax.axis_index("dom")
    return dom >> 3, (dom >> 1) & 3, dom & 1, lax.axis_index("rep")


def sum_share(part):
    _, x, core, rep = place()
    part = rows_of(part, core, 128) + along("core", rows_of(part, 1 - core, 128), 1)
    for axis, me, rows in (("x", x, 32), ("rep", rep, 8)):
        part = rows_of(part, me, rows) + sum(along(axis, rows_of(part, (me + by) & 3, rows), by) for by in (1, 2, 3))
    return part


def sum_z(part):
    for by in (1, 2, 4):
        part = part + along("z", part, by)
    return part


def gather_shares(part):
    _, x, core, rep = place()
    for axis, me in (("rep", rep), ("x", x)):
        part = in_order([part] + [along(axis, part, by) for by in (1, 2, 3)], me)
        part = part.reshape(-1, part.shape[-1])
    other = along("core", part, 1)
    return jnp.where(core == 0, jnp.concatenate([part, other], 0), jnp.concatenate([other, part], 0))


def body(history, batch_ids, halo_ids, halo_counts, adj_local, adj_halo, weight, cotangent):
    owners = lax.axis_size("dom")
    replicas = lax.axis_size("rep")
    rep = lax.axis_index("rep")
    batch_rows = batch_ids.shape[0]
    slots = halo_ids.shape[2]
    width = history.shape[1]
    both = ("dom", "rep")

    asked = exchange(halo_ids.reshape(owners, 1, slots), "dom").reshape(owners * slots)
    fetched = gather_rows(history, asked)
    halo_rows = exchange(fetched.reshape(owners, slots, width), "dom").reshape(owners * slots, width)

    mine = jnp.concatenate([asked, batch_ids]).reshape(-1, 128)
    ids = [mine] + [from_behind(mine, by) for by in (1, 2, 3)]
    asked_rows = owners * slots // 128
    local_ids = jnp.stack([i[asked_rows:] for i in ids], 0).reshape(replicas, 2, batch_rows // 2)
    by_rep = in_order([i[:asked_rows] for i in ids], rep)
    halo_asked = by_rep.reshape(replicas, owners, 2, slots // 2).transpose(2, 1, 0, 3).reshape(-1)
    local_ids = local_ids.transpose(1, 0, 2).reshape(-1)
    halo_rows, *chosen = lax.optimization_barrier(
        (halo_rows, picks(local_ids), lows(local_ids), picks(halo_asked), lows(halo_asked))
    )

    inputs = gather_rows(history, batch_ids)
    local = jnp.dot(adj_local, inputs, preferred_element_type=F32)
    like = jax.ShapeDtypeStruct
    layer_out, weight_part, grad_agg, messages = vmem_call(
        middle_kernel,
        (
            like((batch_rows, width), BF16),
            like((width, width), F32),
            like((batch_rows, width), BF16),
            like((owners * replicas, 16, 128), BF16),
        ),
        [SMEM] + [VMEM] * 5,
        flops=2 * 5 * 2**20 * width,
        moved=8 * 2**20,
        scratch=[pltpu.VMEM((owners * slots, width), BF16)] + [pltpu.VMEM((batch_rows, width), BF16)] * 2,
    )(halo_counts, halo_rows, adj_halo, local, weight, cotangent)
    arrived = exchange(messages, both).reshape(owners * replicas * 16, 128)
    weight_share = sum_z(sum_share(weight_part))
    locals_ = vmem_call(
        local_kernel,
        (like((batch_rows // 2, 128), BF16),) * replicas,
        [SMEM, VMEM, VMEM],
        flops=2 * batch_rows * batch_rows * width,
        moved=3 * 2**20,
        scratch=[pltpu.VMEM((batch_rows, width), F32)],
    )(rep.reshape(1), adj_local, grad_agg)
    locals_ = [locals_[0]] + [from_behind(locals_[by], by) for by in (1, 2, 3)]
    started = vmem_call(
        scatter_local_kernel,
        like((512, 256), F32),
        [VMEM] * 6,
        flops=2 * 4096 * 512 * 256,
        moved=4 * 2**20,
        scratch=[pltpu.VMEM((4096, 256), BF16)],
    )(chosen[0], chosen[1], *locals_)
    arrived, weight_share = lax.optimization_barrier((arrived, weight_share))
    weight_sum = gather_shares(weight_share)
    table = vmem_call(
        scatter_halo_kernel,
        like((512, 256), BF16),
        [VMEM] * 4,
        flops=2 * 8192 * 512 * 256,
        moved=6 * 2**20,
        scratch=[pltpu.VMEM((8192, 256), BF16)],
    )(chosen[2], chosen[3], arrived, started)
    tables = [table] + [from_behind(table, by) for by in (1, 2, 3)]
    history_grad = vmem_call(
        unpack_kernel,
        jax.ShapeDtypeStruct(history.shape, F32),
        [SMEM] + [VMEM] * 4,
        moved=4 * 2**20,
    )(rep.reshape(1), *tables)

    total_rows = batch_rows * owners * replicas
    grad_weight = weight_sum / jnp.sqrt(jnp.float32(total_rows))
    return (layer_out, grad_weight, history_grad)


def solution(mesh):
    return jax.shard_map(
        body,
        mesh=mesh,
        in_specs=(
            P("dom", None),
            P(("dom", "rep")),
            P(("dom", "rep"), None, None),
            P(("dom", "rep"), None),
            P(("dom", "rep"), None),
            P(("dom", "rep"), None),
            P(),
            P(("dom", "rep"), None),
        ),
        out_specs=(P(("dom", "rep"), None), P(), P("dom", None)),
        check_vma=False,
    )
```

```python
import jax
import jax.numpy as jnp
from jax import lax
from jax.experimental import pallas as pl
from jax.experimental.pallas import tpu as pltpu
from jax.sharding import PartitionSpec as P

BF16, F32, I32 = jnp.bfloat16, jnp.float32, jnp.int32
VMEM = pl.BlockSpec(memory_space=pltpu.VMEM)
SMEM = pl.BlockSpec(memory_space=pltpu.SMEM)
ANY = pl.BlockSpec(memory_space=pl.ANY)


def vmem_call(kernel, out_shape, in_specs, flops=0, moved=0, scratch=()):
    return pl.pallas_call(
        kernel,
        out_shape=out_shape,
        in_specs=in_specs,
        out_specs=jax.tree.map(lambda _: VMEM, out_shape),
        scratch_shapes=list(scratch),
        compiler_params=pltpu.CompilerParams(vmem_limit_bytes=16 * 1024 * 1024),
        cost_estimate=pl.CostEstimate(flops=flops, bytes_accessed=moved, transcendentals=0),
    )


def spread_column(columns, i):
    return jnp.broadcast_to(columns[:, i : i + 1], (columns.shape[0], 128))


def gather_kernel(ids_ref, table_ref, out_ref):
    nodes, (groups, size) = table_ref.shape[0], ids_ref.shape
    columns = ids_ref[...].T
    lane = lax.broadcasted_iota(I32, (256, 128), 1)
    for step in range(out_ref.shape[0] // 256):
        many = 256 // size
        column = jnp.concatenate([spread_column(columns, step * many + i) for i in range(many)], 0)
        picks = jnp.concatenate(
            [jnp.where(column == lane + base, 1.0, 0.0).astype(BF16) for base in range(0, nodes, 128)], 1
        )
        rows = jnp.dot(picks, table_ref[...], preferred_element_type=F32)
        out_ref[256 * step : 256 * step + 256, :] = rows.astype(BF16)


def gather_rows(table, ids):
    count, (nodes, width) = ids.size, table.shape
    return vmem_call(
        gather_kernel,
        jax.ShapeDtypeStruct((count, width), BF16),
        [VMEM, VMEM],
        flops=2 * count * nodes * width,
        moved=4 * count * width,
    )(ids, table)


def pack_pair(first, second, part):
    block = slice(128 * (part // 2), 128 * (part // 2) + 128)
    left = lax.broadcasted_iota(I32, (first.shape[0], 128), 1) < 64
    if part % 2 == 0:
        return jnp.where(left, first[:, block], pltpu.roll(second[:, block], 64, 1))
    return jnp.where(left, pltpu.roll(first[:, block], 64, 1), second[:, block])


def middle_kernel(
    counts_ref, rep_ref, rows_hbm, adj_hbm, local_hbm, weight_hbm, cotangent_hbm, adj_local_hbm,
    out_hbm, part_hbm, messages_hbm, *refs,
):
    local_hbms, refs = refs[:4], refs[4:]
    rows_ref, adj_ref, local_ref, weight_ref, cotangent_ref, adj_local_ref, *refs = refs
    out_ref, part_ref, packed_ref, parts_ref, live_ref, agg_ref, grad_pre_ref, grads_ref, sums_ref, load_sems, store_sems = refs
    slots, owners = 32, 64
    half = sums_ref.shape[0] // 2
    chunks = [slice(base, base + 256) for base in range(0, 2 * half, 256)]

    loads, stores = [], []

    def load(source, target):
        loads.append(pltpu.make_async_copy(source, target, load_sems.at[len(loads)]))
        loads[-1].start()
        return loads[-1]

    def store(source, target):
        stores.append(pltpu.make_async_copy(source, target, store_sems.at[len(stores)]))
        stores[-1].start()

    rows_in = load(rows_hbm, rows_ref)
    adj_in = [load(adj_hbm.at[chunks[0]], adj_ref.at[chunks[0]])]
    weight_in, local_in = load(weight_hbm, weight_ref), load(local_hbm, local_ref)
    cotangent_in = load(cotangent_hbm, cotangent_ref)
    adj_in += [load(adj_hbm.at[at], adj_ref.at[at]) for at in chunks[1:]]
    adj_local_in = load(adj_local_hbm, adj_local_ref)

    slot = lax.broadcasted_iota(I32, (slots, 256), 0)
    rows_in.wait()
    for owner in range(owners):
        at = slice(slots * owner, slots * owner + slots)
        live = jnp.where(slot < counts_ref[0, owner], rows_ref[at, :].astype(F32), 0.0)
        live_ref[at, :] = live.astype(BF16)
    for i, at in enumerate(chunks):
        adj_in[i].wait()
        if i == 0:
            weight_in.wait()
            local_in.wait()
            cotangent_in.wait()
        summed = local_ref[at, :] + jnp.dot(adj_ref[at, :], live_ref[...], preferred_element_type=F32)
        agg = summed.astype(BF16)
        agg_ref[at, :] = agg
        pre_act = jnp.dot(agg, weight_ref[...], preferred_element_type=F32)
        gate = jax.nn.sigmoid(pre_act)
        out_ref[at, :] = (pre_act * gate).astype(BF16)
        grad_pre = (cotangent_ref[at, :].astype(F32) * gate * (1.0 + pre_act * (1.0 - gate))).astype(BF16)
        grad_pre_ref[at, :] = grad_pre
        grads_ref[at, :] = lax.dot_general(
            grad_pre, weight_ref[...], (((1,), (1,)), ((), ())), preferred_element_type=F32
        ).astype(BF16)
    store(out_ref, out_hbm)
    for group in range(owners // 8):
        grads = lax.dot_general(
            adj_ref[:, 256 * group : 256 * group + 256],
            grads_ref[...],
            (((0,), (0,)), ((), ())),
            preferred_element_type=F32,
        )
        for step in range(8):
            owner = 8 * group + step
            one = jnp.where(slot < counts_ref[0, owner], grads[slots * step : slots * step + slots], 0.0)
            for part in range(4):
                packed_ref[owner * 4 + part] = pack_pair(one[:16], one[16:], part).astype(BF16)
        at = pl.ds(32 * group, 32)
        store(packed_ref.at[at], messages_hbm.at[at])
    part_ref[...] = lax.dot_general(
        agg_ref[...], grad_pre_ref[...], (((0,), (0,)), ((), ())), preferred_element_type=F32
    )
    store(part_ref, part_hbm)
    adj_local_in.wait()
    for at in chunks:
        sums_ref[at, :] = lax.dot_general(
            adj_local_ref[:, at], grads_ref[...], (((0,), (0,)), ((), ())), preferred_element_type=F32
        )
    for rep in range(4):

        @pl.when(rep_ref[0] == rep)
        def _(rep=rep):
            for base in range(0, half, 128):
                first, second = sums_ref[base : base + 128, :], sums_ref[half + base : half + base + 128, :]
                for part in range(4):
                    parts_ref[part ^ rep, base : base + 128, :] = pack_pair(first, second, part).astype(BF16)

    for i, local_hbm in enumerate(local_hbms):
        store(parts_ref.at[i], local_hbm)
    for copy in stores:
        copy.wait()


def add_rows(total, high, columns, second, packed):
    row = lax.broadcasted_iota(I32, (512, 128), 0)
    left = lax.broadcasted_iota(I32, (128, 128), 1) < 64
    group = jnp.where(left, 0, 1)
    blocks = packed.shape[0] // 128
    picks, spread = [[], []], [[], []]
    for i in range(blocks):
        wide = packed[128 * i : 128 * i + 128, :].astype(F32)
        turned = pltpu.roll(wide, 64, 1)
        for side, rows in enumerate((jnp.where(left, wide, turned), jnp.where(left, turned, wide))):
            at = i + second * side
            low = spread_column(columns, at)
            spread[side].append(
                jnp.concatenate(
                    [jnp.where(low == group, rows, 0.0), jnp.where(low == group + 2, rows, 0.0)], 1
                ).astype(BF16)
            )
            picks[side].append(jnp.where(row == high[at : at + 1, :], 1.0, 0.0).astype(BF16))
    return total + jnp.dot(
        jnp.concatenate(picks[0] + picks[1], 1),
        jnp.concatenate(spread[0] + spread[1], 0),
        preferred_element_type=F32,
    )


def scatter_local_kernel(ids_ref, *refs):
    packed_refs, out_ref = refs[:4], refs[4]
    ids = ids_ref[...]
    high, columns = ids & 511, (ids >> 9).T
    total = jnp.zeros((512, 256), F32)
    for i, packed_ref in enumerate(packed_refs):
        total = add_rows(total, high[4 * i :], columns[:, 4 * i :], 16, packed_ref[...])
    out_ref[...] = total


def scatter_halo_kernel(ids_ref, packed_ref, start_ref, out_ref):
    ids = ids_ref[...]
    high, columns = ids & 511, (ids >> 9).T
    total = start_ref[...]
    for i in range(4):
        packed = packed_ref[1024 * i : 1024 * i + 1024, :]
        total = add_rows(total, high[8 * i :], columns[:, 8 * i :], 32, packed)
    out_ref[...] = total.astype(BF16)


def unpack_kernel(rep_ref, *refs):
    tables, out_ref = refs[:4], refs[4]
    left = lax.broadcasted_iota(I32, (128, 128), 1) < 64
    for rep in range(4):

        @pl.when(rep_ref[0] == rep)
        def _(rep=rep):
            for low in range(4):
                for base in range(0, 512, 128):
                    block = [
                        tables[(rep - part) % 4][base : base + 128, 128 * (low // 2) : 128 * (low // 2) + 128].astype(F32)
                        for part in range(4)
                    ]
                    for pair in range(2):
                        one, two = block[2 * pair], block[2 * pair + 1]
                        if low % 2 == 0:
                            joined = jnp.where(left, one, pltpu.roll(two, 64, 1))
                        else:
                            joined = jnp.where(left, pltpu.roll(one, 64, 1), two)
                        out_ref[512 * low + base : 512 * low + base + 128, 128 * pair : 128 * pair + 128] = joined


def exchange(x, axes):
    return lax.all_to_all(x, axes, split_axis=0, concat_axis=0, tiled=True)


def from_behind(x, by):
    return lax.ppermute(x, "rep", [(i, (i + by) % 4) for i in range(4)])


def rows_of(x, index, rows):
    return lax.dynamic_slice_in_dim(x, index * rows, rows, 0)


def swap(x, axis, bit):
    return lax.ppermute(x, axis, [(i, i ^ bit) for i in range(lax.axis_size(axis))])


HALVES = (("dom", 1), ("dom", 2), ("dom", 4), ("rep", 1), ("rep", 2))


def sum_share(part):
    for axis, bit in HALVES:
        mine = jnp.where(lax.axis_index(axis) & bit != 0, 1, 0)
        rows = part.shape[0] // 2
        part = rows_of(part, mine, rows) + swap(rows_of(part, 1 - mine, rows), axis, bit)
    for bit in (8, 16, 32):
        part = part + swap(part, "dom", bit)
    return part


def joined(part, other, upper):
    return jnp.where(upper, jnp.concatenate([other, part], 0), jnp.concatenate([part, other], 0))


def gather_shares(part):
    for axis, bit in HALVES[::-1]:
        part = joined(part, swap(part, axis, bit), lax.axis_index(axis) & bit != 0)
    return part


def body(history, batch_ids, halo_ids, halo_counts, adj_local, adj_halo, weight, cotangent):
    owners = lax.axis_size("dom")
    replicas = lax.axis_size("rep")
    rep = lax.axis_index("rep")
    batch_rows = batch_ids.shape[0]
    slots = halo_ids.shape[2]
    width = history.shape[1]
    both = ("dom", "rep")

    asked = exchange(halo_ids.reshape(owners, 1, slots), "dom").reshape(owners, slots)
    fetched = gather_rows(history, asked)
    halo_rows = exchange(fetched.reshape(owners, slots, width), "dom").reshape(owners * slots, width)

    near = batch_ids.reshape(1, 2, batch_rows // 2)
    far = asked.reshape(1, owners, 2, slots // 2)
    for bit in (1, 2):
        both_ids = jnp.concatenate([near.reshape(-1), far.reshape(-1)]).reshape(-1, 128)
        other = swap(both_ids, "rep", bit).reshape(-1)
        near = jnp.concatenate([near, other[: near.size].reshape(near.shape)], 0)
        far = joined(far, other[near.size // 2 :].reshape(far.shape), rep & bit != 0)
    local_ids = near.transpose(1, 0, 2).reshape(-1, 128)
    asked_ids = far.transpose(2, 1, 0, 3).reshape(-1, 128)
    halo_rows, local_ids, asked_ids = lax.optimization_barrier((halo_rows, local_ids, asked_ids))

    inputs = gather_rows(history, batch_ids.reshape(-1, 128))
    local = jnp.dot(adj_local, inputs, preferred_element_type=F32)
    like = jax.ShapeDtypeStruct
    rep_of = rep.reshape(1)
    layer_out, weight_part, messages, *locals_ = pl.pallas_call(
        middle_kernel,
        out_shape=(
            like((batch_rows, width), BF16),
            like((width, width), F32),
            like((owners * replicas, slots // 2, 128), BF16),
        )
        + (like((batch_rows // 2, 128), BF16),) * replicas,
        in_specs=[SMEM, SMEM] + [ANY] * 6,
        out_specs=(ANY,) * (3 + replicas),
        scratch_shapes=[pltpu.VMEM(a.shape, a.dtype) for a in (halo_rows, adj_halo, local, weight, cotangent, adj_local)]
        + [
            pltpu.VMEM((batch_rows, width), BF16),
            pltpu.VMEM((width, width), F32),
            pltpu.VMEM((owners * replicas, slots // 2, 128), BF16),
            pltpu.VMEM((replicas, batch_rows // 2, 128), BF16),
            pltpu.VMEM((owners * slots, width), BF16),
            pltpu.VMEM((batch_rows, width), BF16),
            pltpu.VMEM((batch_rows, width), BF16),
            pltpu.VMEM((batch_rows, width), BF16),
            pltpu.VMEM((batch_rows, width), F32),
            pltpu.SemaphoreType.DMA((5 + batch_rows // 256,)),
            pltpu.SemaphoreType.DMA((2 + replicas + owners // 8,)),
        ],
        compiler_params=pltpu.CompilerParams(vmem_limit_bytes=56 * 1024 * 1024),
        cost_estimate=pl.CostEstimate(flops=2 * 7 * 2**20 * width, bytes_accessed=10 * 2**20, transcendentals=0),
    )(halo_counts, rep_of, halo_rows, adj_halo, local, weight, cotangent, adj_local)
    arrived = exchange(messages, both).reshape(owners * replicas * slots // 2, 128)
    weight_share = sum_share(weight_part)
    locals_ = [locals_[0]] + [swap(locals_[bits], "rep", bits) for bits in (1, 2, 3)]
    started = vmem_call(
        scatter_local_kernel,
        like((512, 256), F32),
        [VMEM] * 5,
        flops=2 * 4096 * 512 * 256,
        moved=4 * 2**20,
    )(local_ids, *locals_)
    arrived, weight_share, started = lax.optimization_barrier((arrived, weight_share, started))
    weight_sum = gather_shares(weight_share)
    table = vmem_call(
        scatter_halo_kernel,
        like((512, 256), BF16),
        [VMEM] * 3,
        flops=2 * 8192 * 512 * 256,
        moved=6 * 2**20,
    )(asked_ids, arrived, started)
    tables = [table] + [from_behind(table, by) for by in (1, 2, 3)]
    history_grad = vmem_call(
        unpack_kernel,
        like(history.shape, F32),
        [SMEM] + [VMEM] * 4,
        moved=4 * 2**20,
    )(rep_of, *tables)

    total_rows = batch_rows * owners * replicas
    grad_weight = weight_sum / jnp.sqrt(jnp.float32(total_rows))
    return (layer_out, grad_weight, history_grad)


def solution(mesh):
    return jax.shard_map(
        body,
        mesh=mesh,
        in_specs=(
            P("dom", None),
            P(("dom", "rep")),
            P(("dom", "rep"), None, None),
            P(("dom", "rep"), None),
            P(("dom", "rep"), None),
            P(("dom", "rep"), None),
            P(),
            P(("dom", "rep"), None),
        ),
        out_specs=(P(("dom", "rep"), None), P(), P("dom", None)),
        check_vma=False,
    )
```

```python
import jax
import jax.numpy as jnp
from jax import lax
from jax.experimental import pallas as pl
from jax.experimental.pallas import tpu as pltpu
from jax.sharding import PartitionSpec as P

BF16, F32, I32 = jnp.bfloat16, jnp.float32, jnp.int32
VMEM = pl.BlockSpec(memory_space=pltpu.VMEM)
SMEM = pl.BlockSpec(memory_space=pltpu.SMEM)
ANY = pl.BlockSpec(memory_space=pltpu.HBM)


def vmem_call(kernel, out_shape, in_specs, flops=0, moved=0, scratch=(), mib=16):
    return pl.pallas_call(
        kernel,
        out_shape=out_shape,
        in_specs=in_specs,
        out_specs=jax.tree.map(lambda _: VMEM, out_shape),
        scratch_shapes=list(scratch),
        compiler_params=pltpu.CompilerParams(vmem_limit_bytes=mib * 2**20),
        cost_estimate=pl.CostEstimate(flops=flops, bytes_accessed=moved, transcendentals=0),
    )


def spread_column(columns, i):
    return jnp.broadcast_to(columns[:, i : i + 1], (columns.shape[0], 128))


def gather_kernel(ids_ref, table_ref, out_ref):
    nodes, (groups, size) = table_ref.shape[0], ids_ref.shape
    columns = ids_ref[...].T
    lane = lax.broadcasted_iota(I32, (256, 128), 1)
    for step in range(out_ref.shape[0] // 256):
        many = 256 // size
        column = jnp.concatenate([spread_column(columns, step * many + i) for i in range(many)], 0)
        picks = jnp.concatenate(
            [jnp.where(column == lane + base, 1.0, 0.0).astype(BF16) for base in range(0, nodes, 128)], 1
        )
        rows = jnp.dot(picks, table_ref[...], preferred_element_type=F32)
        out_ref[256 * step : 256 * step + 256, :] = rows.astype(BF16)


def gather_rows(table, ids):
    count, (nodes, width) = ids.size, table.shape
    return vmem_call(
        gather_kernel,
        jax.ShapeDtypeStruct((count, width), BF16),
        [VMEM, VMEM],
        flops=2 * count * nodes * width,
        moved=4 * count * width,
    )(ids, table)


def pack_pair(first, second, part):
    block = slice(128 * (part // 2), 128 * (part // 2) + 128)
    left = lax.broadcasted_iota(I32, (first.shape[0], 128), 1) < 64
    if part % 2 == 0:
        return jnp.where(left, first[:, block], pltpu.roll(second[:, block], 64, 1))
    return jnp.where(left, pltpu.roll(first[:, block], 64, 1), second[:, block])


def middle_kernel(
    counts_hbm, rows_ref, adj_hbm, local_hbm, weight_hbm, cotangent_hbm, adj_local_hbm,
    out_hbm, part_hbm, messages_hbm, *refs,
):
    local_hbms, refs = refs[:4], refs[4:]
    counts_ref, adj_ref, local_ref, weight_ref, cotangent_ref, adj_local_ref, *refs = refs
    out_ref, part_ref, packed_ref, parts_ref, live_ref, agg_ref, grad_pre_ref, grads_ref, sums_ref, load_sems, store_sems = refs
    slots, owners = 32, 64
    half = sums_ref.shape[0] // 2
    chunks = [slice(base, base + 256) for base in range(0, 2 * half, 256)]

    loads, stores = [], []

    def load(source, target):
        loads.append(pltpu.make_async_copy(source, target, load_sems.at[len(loads)]))
        loads[-1].start()
        return loads[-1]

    def store(source, target):
        stores.append(pltpu.make_async_copy(source, target, store_sems.at[len(stores)]))
        stores[-1].start()

    counts_in = load(counts_hbm, counts_ref)
    adj_in = [load(adj_hbm.at[chunks[0]], adj_ref.at[chunks[0]])]
    weight_in, local_in = load(weight_hbm, weight_ref), load(local_hbm, local_ref)
    cotangent_in = load(cotangent_hbm, cotangent_ref)
    adj_in += [load(adj_hbm.at[at], adj_ref.at[at]) for at in chunks[1:]]
    adj_local_in = load(adj_local_hbm, adj_local_ref)

    slot = lax.broadcasted_iota(I32, (slots, 256), 0)
    counts_in.wait()
    for owner in range(owners):
        at = slice(slots * owner, slots * owner + slots)
        live = jnp.where(slot < counts_ref[0, owner], rows_ref[at, :].astype(F32), 0.0)
        live_ref[at, :] = live.astype(BF16)
    for i, at in enumerate(chunks):
        adj_in[i].wait()
        if i == 0:
            weight_in.wait()
            local_in.wait()
            cotangent_in.wait()
        summed = local_ref[at, :] + jnp.dot(adj_ref[at, :], live_ref[...], preferred_element_type=F32)
        agg = summed.astype(BF16)
        agg_ref[at, :] = agg
        pre_act = jnp.dot(agg, weight_ref[...], preferred_element_type=F32)
        gate = jax.nn.sigmoid(pre_act)
        out_ref[at, :] = (pre_act * gate).astype(BF16)
        grad_pre = (cotangent_ref[at, :].astype(F32) * gate * (1.0 + pre_act * (1.0 - gate))).astype(BF16)
        grad_pre_ref[at, :] = grad_pre
        grads_ref[at, :] = lax.dot_general(
            grad_pre, weight_ref[...], (((1,), (1,)), ((), ())), preferred_element_type=F32
        ).astype(BF16)
    store(out_ref, out_hbm)
    for group in range(owners // 8):
        grads = lax.dot_general(
            adj_ref[:, 256 * group : 256 * group + 256],
            grads_ref[...],
            (((0,), (0,)), ((), ())),
            preferred_element_type=F32,
        )
        for step in range(8):
            owner = 8 * group + step
            one = jnp.where(slot < counts_ref[0, owner], grads[slots * step : slots * step + slots], 0.0)
            for part in range(4):
                packed_ref[owner * 4 + part] = pack_pair(one[:16], one[16:], part).astype(BF16)
        at = pl.ds(32 * group, 32)
        store(packed_ref.at[at], messages_hbm.at[at])
    part_ref[...] = lax.dot_general(
        agg_ref[...], grad_pre_ref[...], (((0,), (0,)), ((), ())), preferred_element_type=F32
    )
    store(part_ref, part_hbm)
    adj_local_in.wait()
    for at in chunks:
        sums_ref[at, :] = lax.dot_general(
            adj_local_ref[:, at], grads_ref[...], (((0,), (0,)), ((), ())), preferred_element_type=F32
        )
    for rep in range(4):

        @pl.when(lax.axis_index("rep") == rep)
        def _(rep=rep):
            for base in range(0, half, 128):
                first, second = sums_ref[base : base + 128, :], sums_ref[half + base : half + base + 128, :]
                for part in range(4):
                    parts_ref[part ^ rep, base : base + 128, :] = pack_pair(first, second, part).astype(BF16)

    for i, local_hbm in enumerate(local_hbms):
        store(parts_ref.at[i], local_hbm)
    for copy in stores:
        copy.wait()


def add_rows(total, high, columns, second, packed):
    row = lax.broadcasted_iota(I32, (512, 128), 0)
    left = lax.broadcasted_iota(I32, (128, 128), 1) < 64
    group = jnp.where(left, 0, 1)
    blocks = packed.shape[0] // 128
    picks, spread = [[], []], [[], []]
    for i in range(blocks):
        wide = packed[128 * i : 128 * i + 128, :].astype(F32)
        turned = pltpu.roll(wide, 64, 1)
        for side, rows in enumerate((jnp.where(left, wide, turned), jnp.where(left, turned, wide))):
            at = i + second * side
            low = spread_column(columns, at)
            spread[side].append(
                jnp.concatenate(
                    [jnp.where(low == group, rows, 0.0), jnp.where(low == group + 2, rows, 0.0)], 1
                ).astype(BF16)
            )
            picks[side].append(jnp.where(row == high[at : at + 1, :], 1.0, 0.0).astype(BF16))
    return total + jnp.dot(
        jnp.concatenate(picks[0] + picks[1], 1),
        jnp.concatenate(spread[0] + spread[1], 0),
        preferred_element_type=F32,
    )


def scatter_local_kernel(ids_ref, *refs):
    packed_refs, out_ref = refs[:4], refs[4]
    ids = ids_ref[...]
    high, columns = ids & 511, (ids >> 9).T
    total = jnp.zeros((512, 256), F32)
    for i, packed_ref in enumerate(packed_refs):
        total = add_rows(total, high[4 * i :], columns[:, 4 * i :], 16, packed_ref[0:512, :])
    out_ref[...] = total


def scatter_halo_kernel(ids_ref, packed_ref, start_ref, out_ref):
    ids = ids_ref[...]
    high, columns = ids & 511, (ids >> 9).T
    total = start_ref[...]
    for i in range(4):
        packed = packed_ref[1024 * i : 1024 * i + 1024, :]
        total = add_rows(total, high[8 * i :], columns[:, 8 * i :], 32, packed)
    out_ref[...] = total.astype(BF16)


def unpack_kernel(*refs):
    tables, out_ref = refs[:4], refs[4]
    left = lax.broadcasted_iota(I32, (128, 128), 1) < 64
    for rep in range(4):

        @pl.when(lax.axis_index("rep") == rep)
        def _(rep=rep):
            for low in range(4):
                for base in range(0, 512, 128):
                    block = [
                        tables[(rep - part) % 4][base : base + 128, 128 * (low // 2) : 128 * (low // 2) + 128].astype(F32)
                        for part in range(4)
                    ]
                    for pair in range(2):
                        one, two = block[2 * pair], block[2 * pair + 1]
                        if low % 2 == 0:
                            joined = jnp.where(left, one, pltpu.roll(two, 64, 1))
                        else:
                            joined = jnp.where(left, pltpu.roll(one, 64, 1), two)
                        out_ref[512 * low + base : 512 * low + base + 128, 128 * pair : 128 * pair + 128] = joined


def exchange(x, axes):
    return lax.all_to_all(x, axes, split_axis=0, concat_axis=0, tiled=True)


def from_behind(x, by):
    return lax.ppermute(x, "rep", [(i, (i + by) % 4) for i in range(4)])


def rows_of(x, index, rows):
    return lax.dynamic_slice_in_dim(x, index * rows, rows, 0)


def swap(x, axis, bit):
    return lax.ppermute(x, axis, [(i, i ^ bit) for i in range(lax.axis_size(axis))])


def place(axis, bits):
    return lax.axis_index(axis) & bits


def sum_chip_row(part):
    core, x = place("dom", 1), place("dom", 6) >> 1
    part = rows_of(part, core, 128) + swap(rows_of(part, 1 - core, 128), "dom", 1)
    return rows_of(part, x, 32) + sum(swap(rows_of(part, x ^ bits, 32), "dom", 2 * bits) for bits in (1, 2, 3))


def sum_replicas(part):
    others = [swap(part, "rep", bits) for bits in (1, 2, 3)]
    return (part + others[0]) + (others[1] + others[2])


def sum_z(part, bits):
    for bit in bits:
        part = part + swap(part, "dom", bit)
    return part


def joined(part, other, upper):
    return jnp.where(upper, jnp.concatenate([other, part], 0), jnp.concatenate([part, other], 0))


def gather_chip_row(part):
    near = [part] + [swap(part, "dom", 2 * bits) for bits in (1, 2, 3)]
    odd, high = place("dom", 2) != 0, place("dom", 4) != 0
    half = joined(joined(near[0], near[1], odd), joined(near[2], near[3], odd), high)
    return joined(half, swap(half, "dom", 1), place("dom", 1) != 0)


def body(history, batch_ids, halo_ids, halo_counts, adj_local, adj_halo, weight, cotangent):
    owners = lax.axis_size("dom")
    replicas = lax.axis_size("rep")
    rep = lax.axis_index("rep")
    batch_rows = batch_ids.shape[0]
    slots = halo_ids.shape[2]
    width = history.shape[1]
    both = ("dom", "rep")

    asked = exchange(halo_ids.reshape(owners, 1, slots), "dom").reshape(owners, slots)
    fetched = gather_rows(history, asked)
    halo_rows = exchange(fetched.reshape(owners, slots, width), "dom").reshape(owners * slots, width)

    near = batch_ids.reshape(1, 2, batch_rows // 2)
    far = asked.reshape(1, owners, 2, slots // 2)
    for bit in (1, 2):
        both_ids = jnp.concatenate([near.reshape(-1), far.reshape(-1)]).reshape(-1, 128)
        other = swap(both_ids, "rep", bit).reshape(-1)
        near = jnp.concatenate([near, other[: near.size].reshape(near.shape)], 0)
        far = joined(far, other[near.size // 2 :].reshape(far.shape), rep & bit != 0)
    local_ids = near.transpose(1, 0, 2).reshape(-1, 128)
    asked_ids = far.transpose(2, 1, 0, 3).reshape(-1, 128)
    halo_rows, local_ids, asked_ids = lax.optimization_barrier((halo_rows, local_ids, asked_ids))

    inputs = gather_rows(history, batch_ids.reshape(-1, 128))
    local = jnp.dot(adj_local, inputs, preferred_element_type=F32)
    like = jax.ShapeDtypeStruct
    layer_out, weight_part, messages, *locals_ = pl.pallas_call(
        middle_kernel,
        out_shape=(
            like((batch_rows, width), BF16),
            like((width, width), F32),
            like((owners * replicas, slots // 2, 128), BF16),
        )
        + (like((batch_rows // 2, 128), BF16),) * replicas,
        in_specs=[ANY, VMEM] + [ANY] * 5,
        out_specs=(ANY,) * (3 + replicas),
        scratch_shapes=[pltpu.SMEM(halo_counts.shape, I32)]
        + [pltpu.VMEM(a.shape, a.dtype) for a in (adj_halo, local, weight, cotangent, adj_local)]
        + [
            pltpu.VMEM((batch_rows, width), BF16),
            pltpu.VMEM((width, width), F32),
            pltpu.VMEM((owners * replicas, slots // 2, 128), BF16),
            pltpu.VMEM((replicas, batch_rows // 2, 128), BF16),
            pltpu.VMEM((owners * slots, width), BF16),
            pltpu.VMEM((batch_rows, width), BF16),
            pltpu.VMEM((batch_rows, width), BF16),
            pltpu.VMEM((batch_rows, width), BF16),
            pltpu.VMEM((batch_rows, width), F32),
            pltpu.SemaphoreType.DMA((5 + batch_rows // 256,)),
            pltpu.SemaphoreType.DMA((2 + replicas + owners // 8,)),
        ],
        compiler_params=pltpu.CompilerParams(vmem_limit_bytes=56 * 2**20),
        cost_estimate=pl.CostEstimate(flops=2 * 7 * 2**20 * width, bytes_accessed=10 * 2**20, transcendentals=0),
    )(halo_counts, halo_rows, adj_halo, local, weight, cotangent, adj_local)
    arrived = exchange(messages, both).reshape(owners * replicas * slots // 2, 128)
    weight_share = sum_z(sum_replicas(sum_chip_row(weight_part)), (8, 16))
    locals_ = [locals_[0]] + [swap(locals_[bits], "rep", bits) for bits in (1, 2, 3)]
    started = vmem_call(
        scatter_local_kernel,
        like((512, 256), F32),
        [VMEM] * 5,
        moved=2**17,
    )(local_ids, *locals_)
    arrived, started, weight_share = lax.optimization_barrier((arrived, started, weight_share))
    table = vmem_call(
        scatter_halo_kernel,
        like((512, 256), BF16),
        [VMEM] * 3,
        flops=2 * 8192 * 512 * 256,
        moved=6 * 2**20,
    )(asked_ids, arrived, started)
    weight_share = sum_z(weight_share, (32,))
    table, weight_share = lax.optimization_barrier((table, weight_share))
    weight_sum = gather_chip_row(sum_z(weight_share, ()))
    tables = [table] + [from_behind(table, by) for by in (1, 2, 3)]
    history_grad = vmem_call(
        unpack_kernel,
        like(history.shape, F32),
        [VMEM] * 4,
        moved=4 * 2**20,
    )(*tables)

    total_rows = batch_rows * owners * replicas
    grad_weight = weight_sum / jnp.sqrt(jnp.float32(total_rows))
    return (layer_out, grad_weight, history_grad)


def solution(mesh):
    return jax.shard_map(
        body,
        mesh=mesh,
        in_specs=(
            P("dom", None),
            P(("dom", "rep")),
            P(("dom", "rep"), None, None),
            P(("dom", "rep"), None),
            P(("dom", "rep"), None),
            P(("dom", "rep"), None),
            P(),
            P(("dom", "rep"), None),
        ),
        out_specs=(P(("dom", "rep"), None), P(), P("dom", None)),
        check_vma=False,
    )
```

```python
import jax
import jax.numpy as jnp
from jax import lax
from jax.experimental import pallas as pl
from jax.experimental.pallas import tpu as pltpu
from jax.sharding import PartitionSpec as P

BF16, F32, I32 = jnp.bfloat16, jnp.float32, jnp.int32
VMEM = pl.BlockSpec(memory_space=pltpu.VMEM)
SMEM = pl.BlockSpec(memory_space=pltpu.SMEM)
ANY = pl.BlockSpec(memory_space=pltpu.HBM)


def vmem_call(kernel, out_shape, in_specs, flops=0, moved=0, scratch=(), mib=16):
    return pl.pallas_call(
        kernel,
        out_shape=out_shape,
        in_specs=in_specs,
        out_specs=jax.tree.map(lambda _: VMEM, out_shape),
        scratch_shapes=list(scratch),
        compiler_params=pltpu.CompilerParams(vmem_limit_bytes=mib * 2**20),
        cost_estimate=pl.CostEstimate(flops=flops, bytes_accessed=moved, transcendentals=0),
    )


def spread_column(columns, i):
    return jnp.broadcast_to(columns[:, i : i + 1], (columns.shape[0], 128))


def gather_kernel(ids_ref, table_ref, out_ref):
    nodes, (groups, size) = table_ref.shape[0], ids_ref.shape
    columns = ids_ref[...].T
    lane = lax.broadcasted_iota(I32, (256, 128), 1)
    for step in range(out_ref.shape[0] // 256):
        many = 256 // size
        column = jnp.concatenate([spread_column(columns, step * many + i) for i in range(many)], 0)
        picks = jnp.concatenate(
            [jnp.where(column == lane + base, 1.0, 0.0).astype(BF16) for base in range(0, nodes, 128)], 1
        )
        rows = jnp.dot(picks, table_ref[...], preferred_element_type=F32)
        out_ref[256 * step : 256 * step + 256, :] = rows.astype(BF16)


def gather_rows(table, ids):
    count, (nodes, width) = ids.size, table.shape
    return vmem_call(
        gather_kernel,
        jax.ShapeDtypeStruct((count, width), BF16),
        [VMEM, VMEM],
        flops=2 * count * nodes * width,
        moved=4 * count * width,
    )(ids, table)


def pack_pair(first, second, part):
    block = slice(128 * (part // 2), 128 * (part // 2) + 128)
    left = lax.broadcasted_iota(I32, (first.shape[0], 128), 1) < 64
    if part % 2 == 0:
        return jnp.where(left, first[:, block], pltpu.roll(second[:, block], 64, 1))
    return jnp.where(left, pltpu.roll(first[:, block], 64, 1), second[:, block])


def middle_kernel(
    counts_hbm, rows_ref, adj_hbm, local_hbm, weight_hbm, cotangent_hbm, adj_local_hbm,
    out_hbm, part_hbm, messages_hbm, *refs,
):
    local_hbms, refs = refs[:4], refs[4:]
    counts_ref, adj_ref, local_ref, weight_ref, cotangent_ref, adj_local_ref, *refs = refs
    out_ref, part_ref, packed_ref, parts_ref, live_ref, agg_ref, grad_pre_ref, grads_ref, sums_ref, load_sems, store_sems = refs
    slots, owners = 32, 64
    half = sums_ref.shape[0] // 2
    chunks = [slice(base, base + 256) for base in range(0, 2 * half, 256)]

    loads, stores = [], []

    def load(source, target):
        loads.append(pltpu.make_async_copy(source, target, load_sems.at[len(loads)]))
        loads[-1].start()
        return loads[-1]

    def store(source, target):
        stores.append(pltpu.make_async_copy(source, target, store_sems.at[len(stores)]))
        stores[-1].start()

    counts_in = load(counts_hbm, counts_ref)
    adj_in = [load(adj_hbm.at[chunks[0]], adj_ref.at[chunks[0]])]
    weight_in, local_in = load(weight_hbm, weight_ref), load(local_hbm, local_ref)
    cotangent_in = load(cotangent_hbm, cotangent_ref)
    adj_in += [load(adj_hbm.at[at], adj_ref.at[at]) for at in chunks[1:]]
    adj_local_in = load(adj_local_hbm, adj_local_ref)

    slot = lax.broadcasted_iota(I32, (slots, 256), 0)
    counts_in.wait()
    for owner in range(owners):
        at = slice(slots * owner, slots * owner + slots)
        live = jnp.where(slot < counts_ref[0, owner], rows_ref[at, :].astype(F32), 0.0)
        live_ref[at, :] = live.astype(BF16)
    for i, at in enumerate(chunks):
        adj_in[i].wait()
        if i == 0:
            weight_in.wait()
            local_in.wait()
            cotangent_in.wait()
        summed = local_ref[at, :] + jnp.dot(adj_ref[at, :], live_ref[...], preferred_element_type=F32)
        agg = summed.astype(BF16)
        agg_ref[at, :] = agg
        pre_act = jnp.dot(agg, weight_ref[...], preferred_element_type=F32)
        gate = jax.nn.sigmoid(pre_act)
        out_ref[at, :] = (pre_act * gate).astype(BF16)
        grad_pre = (cotangent_ref[at, :].astype(F32) * gate * (1.0 + pre_act * (1.0 - gate))).astype(BF16)
        grad_pre_ref[at, :] = grad_pre
        grads_ref[at, :] = lax.dot_general(
            grad_pre, weight_ref[...], (((1,), (1,)), ((), ())), preferred_element_type=F32
        ).astype(BF16)
    store(out_ref, out_hbm)
    for group in range(owners // 8):
        grads = lax.dot_general(
            adj_ref[:, 256 * group : 256 * group + 256],
            grads_ref[...],
            (((0,), (0,)), ((), ())),
            preferred_element_type=F32,
        )
        for step in range(8):
            owner = 8 * group + step
            one = jnp.where(slot < counts_ref[0, owner], grads[slots * step : slots * step + slots], 0.0)
            for part in range(4):
                packed_ref[owner * 4 + part] = pack_pair(one[:16], one[16:], part).astype(BF16)
        at = pl.ds(32 * group, 32)
        store(packed_ref.at[at], messages_hbm.at[at])
    part_ref[...] = lax.dot_general(
        agg_ref[...], grad_pre_ref[...], (((0,), (0,)), ((), ())), preferred_element_type=F32
    )
    store(part_ref, part_hbm)
    adj_local_in.wait()
    for at in chunks:
        sums_ref[at, :] = lax.dot_general(
            adj_local_ref[:, at], grads_ref[...], (((0,), (0,)), ((), ())), preferred_element_type=F32
        )
    for rep in range(4):

        @pl.when(lax.axis_index("rep") == rep)
        def _(rep=rep):
            for base in range(0, half, 128):
                first, second = sums_ref[base : base + 128, :], sums_ref[half + base : half + base + 128, :]
                for part in range(4):
                    parts_ref[part ^ rep, base : base + 128, :] = pack_pair(first, second, part).astype(BF16)

    for i, local_hbm in enumerate(local_hbms):
        store(parts_ref.at[i], local_hbm)
    for copy in stores:
        copy.wait()


def add_rows(total, high, columns, second, packed):
    row = lax.broadcasted_iota(I32, (512, 128), 0)
    left = lax.broadcasted_iota(I32, (128, 128), 1) < 64
    group = jnp.where(left, 0, 1)
    blocks = packed.shape[0] // 128
    picks, spread = [[], []], [[], []]
    for i in range(blocks):
        wide = packed[128 * i : 128 * i + 128, :].astype(F32)
        turned = pltpu.roll(wide, 64, 1)
        for side, rows in enumerate((jnp.where(left, wide, turned), jnp.where(left, turned, wide))):
            at = i + second * side
            low = spread_column(columns, at)
            spread[side].append(
                jnp.concatenate(
                    [jnp.where(low == group, rows, 0.0), jnp.where(low == group + 2, rows, 0.0)], 1
                ).astype(BF16)
            )
            picks[side].append(jnp.where(row == high[at : at + 1, :], 1.0, 0.0).astype(BF16))
    return total + jnp.dot(
        jnp.concatenate(picks[0] + picks[1], 1),
        jnp.concatenate(spread[0] + spread[1], 0),
        preferred_element_type=F32,
    )


def scatter_local_kernel(ids_ref, *refs):
    packed_refs, out_ref = refs[:4], refs[4]
    ids = ids_ref[...]
    high, columns = ids & 511, (ids >> 9).T
    total = jnp.zeros((512, 256), F32)
    for i, packed_ref in enumerate(packed_refs):
        total = add_rows(total, high[4 * i :], columns[:, 4 * i :], 16, packed_ref[0:512, :])
    out_ref[...] = total


def scatter_halo_kernel(ids_ref, packed_ref, start_ref, out_ref):
    ids = ids_ref[...]
    high, columns = ids & 511, (ids >> 9).T
    total = start_ref[...]
    for i in range(4):
        packed = packed_ref[1024 * i : 1024 * i + 1024, :]
        total = add_rows(total, high[8 * i :], columns[:, 8 * i :], 32, packed)
    out_ref[...] = total.astype(BF16)


def unpack_kernel(*refs):
    tables, out_ref = refs[:4], refs[4]
    left = lax.broadcasted_iota(I32, (128, 128), 1) < 64
    for rep in range(4):

        @pl.when(lax.axis_index("rep") == rep)
        def _(rep=rep):
            for low in range(4):
                for base in range(0, 512, 128):
                    block = [
                        tables[(rep - part) % 4][base : base + 128, 128 * (low // 2) : 128 * (low // 2) + 128].astype(F32)
                        for part in range(4)
                    ]
                    for pair in range(2):
                        one, two = block[2 * pair], block[2 * pair + 1]
                        if low % 2 == 0:
                            joined = jnp.where(left, one, pltpu.roll(two, 64, 1))
                        else:
                            joined = jnp.where(left, pltpu.roll(one, 64, 1), two)
                        out_ref[512 * low + base : 512 * low + base + 128, 128 * pair : 128 * pair + 128] = joined


def exchange(x, axes):
    return lax.all_to_all(x, axes, split_axis=0, concat_axis=0, tiled=True)


def from_behind(x, by):
    return lax.ppermute(x, "rep", [(i, (i + by) % 4) for i in range(4)])


def rows_of(x, index, rows):
    return lax.dynamic_slice_in_dim(x, index * rows, rows, 0)


def swap(x, axis, bit):
    return lax.ppermute(x, axis, [(i, i ^ bit) for i in range(lax.axis_size(axis))])


def place(axis, bits):
    return lax.axis_index(axis) & bits


def sum_chip_row(part):
    core, x = place("dom", 1), place("dom", 6) >> 1
    part = rows_of(part, core, 128) + swap(rows_of(part, 1 - core, 128), "dom", 1)
    return rows_of(part, x, 32) + sum(swap(rows_of(part, x ^ bits, 32), "dom", 2 * bits) for bits in (1, 2, 3))


def sum_replicas(part):
    others = [swap(part, "rep", bits) for bits in (1, 2, 3)]
    return (part + others[0]) + (others[1] + others[2])


def sum_z(part, bits):
    for bit in bits:
        part = part + swap(part, "dom", bit)
    return part


def joined(part, other, upper):
    return jnp.where(upper, jnp.concatenate([other, part], 0), jnp.concatenate([part, other], 0))


def gather_chip_row(part):
    near = [part] + [swap(part, "dom", 2 * bits) for bits in (1, 2, 3)]
    odd, high = place("dom", 2) != 0, place("dom", 4) != 0
    half = joined(joined(near[0], near[1], odd), joined(near[2], near[3], odd), high)
    return joined(half, swap(half, "dom", 1), place("dom", 1) != 0)


def body(history, batch_ids, halo_ids, halo_counts, adj_local, adj_halo, weight, cotangent):
    owners = lax.axis_size("dom")
    replicas = lax.axis_size("rep")
    rep = lax.axis_index("rep")
    batch_rows = batch_ids.shape[0]
    slots = halo_ids.shape[2]
    width = history.shape[1]
    both = ("dom", "rep")

    asked = exchange(halo_ids.reshape(owners, 1, slots), "dom").reshape(owners, slots)
    fetched = gather_rows(history, asked)
    halo_rows = exchange(fetched.reshape(owners, slots, width), "dom").reshape(owners * slots, width)

    near = batch_ids.reshape(1, 2, batch_rows // 2)
    far = asked.reshape(1, owners, 2, slots // 2)
    for bit in (1, 2):
        both_ids = jnp.concatenate([near.reshape(-1), far.reshape(-1)]).reshape(-1, 128)
        other = swap(both_ids, "rep", bit).reshape(-1)
        near = jnp.concatenate([near, other[: near.size].reshape(near.shape)], 0)
        far = joined(far, other[near.size // 2 :].reshape(far.shape), rep & bit != 0)
    local_ids = near.transpose(1, 0, 2).reshape(-1, 128)
    asked_ids = far.transpose(2, 1, 0, 3).reshape(-1, 128)
    halo_rows, local_ids, asked_ids = lax.optimization_barrier((halo_rows, local_ids, asked_ids))

    inputs = gather_rows(history, batch_ids.reshape(-1, 128))
    local = jnp.dot(adj_local, inputs, preferred_element_type=F32)
    like = jax.ShapeDtypeStruct
    layer_out, weight_part, messages, *locals_ = pl.pallas_call(
        middle_kernel,
        out_shape=(
            like((batch_rows, width), BF16),
            like((width, width), F32),
            like((owners * replicas, slots // 2, 128), BF16),
        )
        + (like((batch_rows // 2, 128), BF16),) * replicas,
        in_specs=[ANY, VMEM] + [ANY] * 5,
        out_specs=(ANY,) * (3 + replicas),
        scratch_shapes=[pltpu.SMEM(halo_counts.shape, I32)]
        + [pltpu.VMEM(a.shape, a.dtype) for a in (adj_halo, local, weight, cotangent, adj_local)]
        + [
            pltpu.VMEM((batch_rows, width), BF16),
            pltpu.VMEM((width, width), F32),
            pltpu.VMEM((owners * replicas, slots // 2, 128), BF16),
            pltpu.VMEM((replicas, batch_rows // 2, 128), BF16),
            pltpu.VMEM((owners * slots, width), BF16),
            pltpu.VMEM((batch_rows, width), BF16),
            pltpu.VMEM((batch_rows, width), BF16),
            pltpu.VMEM((batch_rows, width), BF16),
            pltpu.VMEM((batch_rows, width), F32),
            pltpu.SemaphoreType.DMA((5 + batch_rows // 256,)),
            pltpu.SemaphoreType.DMA((2 + replicas + owners // 8,)),
        ],
        compiler_params=pltpu.CompilerParams(vmem_limit_bytes=50 * 2**20),
        cost_estimate=pl.CostEstimate(flops=2 * 7 * 2**20 * width, bytes_accessed=10 * 2**20, transcendentals=0),
    )(halo_counts, halo_rows, adj_halo, local, weight, cotangent, adj_local)
    arrived = exchange(messages, both).reshape(owners * replicas * slots // 2, 128)
    weight_share = sum_z(sum_replicas(sum_chip_row(weight_part)), (8, 16))
    locals_ = [locals_[0]] + [swap(locals_[bits], "rep", bits) for bits in (1, 2, 3)]
    started = vmem_call(
        scatter_local_kernel,
        like((512, 256), F32),
        [VMEM] * 5,
        moved=2**17,
    )(local_ids, *locals_)
    arrived, started, weight_share = lax.optimization_barrier((arrived, started, weight_share))
    table = vmem_call(
        scatter_halo_kernel,
        like((512, 256), BF16),
        [VMEM] * 3,
        flops=2 * 8192 * 512 * 256,
        moved=6 * 2**20,
    )(asked_ids, arrived, started)
    weight_share = sum_z(weight_share, (32,))
    table, weight_share = lax.optimization_barrier((table, weight_share))
    weight_sum = gather_chip_row(sum_z(weight_share, ()))
    tables = [table] + [from_behind(table, by) for by in (1, 2, 3)]
    history_grad = vmem_call(
        unpack_kernel,
        like(history.shape, F32),
        [VMEM] * 4,
        moved=4 * 2**20,
    )(*tables)

    total_rows = batch_rows * owners * replicas
    grad_weight = weight_sum / jnp.sqrt(jnp.float32(total_rows))
    return (layer_out, grad_weight, history_grad)


def solution(mesh):
    return jax.shard_map(
        body,
        mesh=mesh,
        in_specs=(
            P("dom", None),
            P(("dom", "rep")),
            P(("dom", "rep"), None, None),
            P(("dom", "rep"), None),
            P(("dom", "rep"), None),
            P(("dom", "rep"), None),
            P(),
            P(("dom", "rep"), None),
        ),
        out_specs=(P(("dom", "rep"), None), P(), P("dom", None)),
        check_vma=False,
    )
```
